32 devices in a mesh: groups: 2 (over y), owner: 4 (over z), head: 4 (over x, core).
Axes of the slice: x: 2, y: 2, z: 4, core: 2. Of those that a mesh axis runs over, the one named last changes fastest.
Arguments:
- tokens: bfloat16 [16384, 1024], P(('groups', 'owner')), parts along dimension 0, may hold values from -12 to 12
- d_out: bfloat16 [16384, 1024], P(('groups', 'owner')), parts along dimension 0, may hold values from -6 to 6
- w_query: bfloat16 [1024, 1024], P(None, 'head'), may hold values from -0.25 to 0.25
- w_key: bfloat16 [1024, 1024], P(None, 'head'), may hold values from -0.25 to 0.25
- w_value: bfloat16 [1024, 1024], P(None, 'head'), may hold values from -0.25 to 0.25
- w_out: bfloat16 [1024, 1024], P('head'), may hold values from -0.1875 to 0.1875
- fetch_list: int32 [8, 4, 4], P(('groups', 'owner')), parts along dimension 0, may hold values from 0 to 15
- fetch_count: int32 [8, 4], P(('groups', 'owner')), parts along dimension 0, may hold values from 0 to 4
- pattern: int32 [128, 8], P(('groups', 'owner')), parts along dimension 0, may hold values from 0 to 31, as said below
Outputs:
- d_tokens: bfloat16 [16384, 1024], P(('groups', 'owner'), 'head'), parts along dimension 0
- grad_query: float32 [2048, 1024], P(('groups', 'owner'), 'head'), parts along dimension 0
- grad_key: float32 [2048, 1024], P(('groups', 'owner'), 'head'), parts along dimension 0
- grad_value: float32 [2048, 1024], P(('groups', 'owner'), 'head'), parts along dimension 0
- grad_out: float32 [2048, 1024], P(('groups', 'head'), 'owner'), parts along dimension 0
The draws below stay inside these ranges and needn't reach their ends.
There are 2 independent parts, one for each index of `groups`. The reference program is written for one: setup_inputs(seed, part) draws one part's arguments, and reference() takes and returns one part's arrays. A program takes and returns all parts, laid end to end along the dimension named above; an argument that names none is the same for every part. Nothing has to cross between parts.
Inputs may be any that keep to these rules, and one draw needn't show every extreme that they name: `pattern`: column 0 of every row names an owner's own block (below 16).
All inputs are finite; a program needn't handle non-finite values.
Results may differ from the reference program's by a relative error of at most 0.018.
The reference program's roundings to bfloat16 on the way (of `grad_attn`, `probs_low`, `attended`, `grad_scores` and `grad_q`) count: a program that leaves them out, or rounds other values in their place, can miss the bound.
Values may be sent and summed in bfloat16 or wider, within the bound.
A program may use at most 192 MiB of HBM per device.

```python
import math
import jax
import jax.numpy as jnp
from jax import lax

D = 1024
HEAD_DIM = 64
BLOCK = 128
BLK_DEV = 16
KMAX = 8
CAP = 4
NBLK = 64
TOKENS = 8192
WSET = 32
N_OWNER = 4


def draw_tokens(key, part):
    key = jax.random.fold_in(key, 3)
    base_key = jax.random.fold_in(key, 0)
    base = jax.random.truncated_normal(base_key, -6.0, 6.0, (TOKENS, D), jnp.float32)
    return base.astype(jnp.bfloat16)


def draw_pattern(key, part):
    key = jax.random.fold_in(key, 5)
    first_key, other_key = jax.random.split(key)
    first = jax.random.randint(first_key, (NBLK, 1), 0, BLK_DEV)
    others = jax.random.randint(other_key, (NBLK, KMAX - 1), 0, WSET)
    return jnp.concatenate([first, others], axis=1).astype(jnp.int32)


def touch_ends(drawn, key, low, largest):
    longest = drawn.shape.index(max(drawn.shape))
    spots = []
    for shift in (0, 1):
        where = [jax.random.randint(jax.random.fold_in(key, axis), (), 0, length) for axis, length in enumerate(drawn.shape)]
        where[longest] = (where[longest] + shift) % drawn.shape[longest]
        spots.append(tuple(where))
    return drawn.at[spots[0]].set(low).at[spots[1]].set(largest)


def spiked(result, own_key, source, target, blocks, factor):
    def block_of(axis_at):
        return (jnp.arange(result.shape[axis_at]) // (result.shape[axis_at] // blocks)).reshape((-1,) + (1,) * (result.ndim - 1 - axis_at))

    near = jax.random.permutation(own_key, blocks)[block_of(target)]
    other_side = (block_of(target) + blocks // 2) % blocks
    return jnp.where((block_of(source) == near) | (block_of(source) == other_side), factor * result, result)


def block_levels(rng, extent, cuts, least, high):
    level, own = 1.0, jax.random.fold_in(rng, 6)
    for axis_at, parts in cuts:
        steps = jnp.exp(jax.random.uniform(jax.random.fold_in(own, axis_at), (parts,), jnp.float32, least / len(cuts), high / len(cuts)))
        level = level * jnp.repeat(steps, extent[axis_at] // parts).reshape([-1 if axis == axis_at else 1 for axis in range(len(extent))])
    return level


def scatter_about(rng, dims, deviation, bound, cuts=(), held_as=jnp.bfloat16):
    drawn = deviation * jax.random.normal(rng, dims, jnp.float32)
    if cuts:
        drawn = drawn * block_levels(rng, dims, cuts, -0.22, 0.18)
    return jnp.clip(drawn, -bound, bound).astype(held_as)


def bell_draw_with(stream_key, dims, deviation, reach, cuts, heavy, kind=jnp.bfloat16):
    drawn = deviation * jax.random.normal(stream_key, dims, jnp.float32)
    if cuts:
        drawn = drawn * block_levels(stream_key, dims, cuts, -0.22, 0.18)
    return jnp.clip(spiked(drawn, jax.random.fold_in(stream_key, 3), *heavy), -reach, reach).astype(kind)


def setup_inputs(seed: int = 0, part: int = 0) -> dict:
    key_list = jax.random.split(jax.random.key(seed), 10)
    part_keys = jax.random.split(jax.random.fold_in(key_list[9], part), 10)
    tokens = draw_tokens(jax.random.fold_in(jax.random.fold_in(key_list[9], part), 71), part)
    d_out = bell_draw_with(part_keys[1], (TOKENS, D), 1.0, 6.0, ((0, 4),), (0, 1, 4, 2.0))
    w_query = bell_draw_with(key_list[2], (D, D), D ** -0.5, 0.25, ((1, 4),), (1, 0, 4, 2.0))
    w_key = bell_draw_with(key_list[3], (D, D), D ** -0.5, 0.25, ((1, 4),), (1, 0, 4, 2.0))
    w_value = bell_draw_with(key_list[4], (D, D), D ** -0.5, 0.25, ((1, 4),), (1, 0, 4, 2.0))
    w_out = scatter_about(key_list[5], (D, D), D ** -0.5, 0.1875, ((0, 4),))
    fetch_list = touch_ends(jax.random.randint(part_keys[6], (N_OWNER, N_OWNER, CAP), 0, BLK_DEV), jax.random.fold_in(part_keys[6], 1), 0, BLK_DEV - 1).astype(jnp.int32)
    fetch_count = touch_ends(jax.random.randint(part_keys[7], (N_OWNER, N_OWNER), 0, CAP + 1), jax.random.fold_in(part_keys[7], 1), 0, CAP).astype(jnp.int32)
    pattern = draw_pattern(jax.random.fold_in(jax.random.fold_in(key_list[9], part), 71), part)
    return {"tokens": tokens, "d_out": d_out, "w_query": w_query, "w_key": w_key, "w_value": w_value, "w_out": w_out, "fetch_list": fetch_list, "fetch_count": fetch_count, "pattern": pattern}


def attend(query_blk, grad_blk, key_rows, value_rows, alive):
    scale = 1.0 / math.sqrt(HEAD_DIM)
    heads = query_blk.shape[1] // HEAD_DIM
    query_h = query_blk.astype(jnp.float32).reshape(BLOCK, heads, HEAD_DIM)
    grad_h = grad_blk.astype(jnp.float32).reshape(BLOCK, heads, HEAD_DIM)
    key_h = key_rows.astype(jnp.float32).reshape(-1, heads, HEAD_DIM)
    value_h = value_rows.astype(jnp.float32).reshape(-1, heads, HEAD_DIM)
    scores = jnp.einsum('thd,shd->hts', query_h, key_h) * scale
    scores = jnp.where(alive[None, None, :], scores, -1e+30)
    probs = jnp.exp(scores - lax.optimization_barrier(jnp.max(scores, axis=-1, keepdims=True)))
    probs = probs / lax.optimization_barrier(jnp.sum(probs, axis=-1, keepdims=True))
    probs_low = lax.optimization_barrier(probs.astype(jnp.bfloat16)).astype(jnp.float32)
    attended = jnp.einsum('hts,shd->thd', probs_low, value_h).astype(jnp.bfloat16)
    row_dot = lax.optimization_barrier(jnp.sum(grad_h * attended.astype(jnp.float32), axis=-1))
    grad_probs = jnp.einsum('thd,shd->hts', grad_h, value_h)
    grad_scores = probs * (grad_probs - jnp.transpose(row_dot)[:, :, None])
    grad_low = lax.optimization_barrier(grad_scores.astype(jnp.bfloat16)).astype(jnp.float32)
    grad_q = jnp.einsum('hts,shd->thd', grad_low, key_h) * scale
    grad_k = jnp.einsum('hts,thd->shd', grad_low, query_h) * scale
    grad_v = jnp.einsum('hts,thd->shd', probs_low, grad_h)
    width = heads * HEAD_DIM
    return (attended.reshape(BLOCK, width), grad_q.reshape(BLOCK, width), grad_k.reshape(-1, width), grad_v.reshape(-1, width))

def reference(tokens, d_out, w_query, w_key, w_value, w_out, fetch_list, fetch_count, pattern):
    query = jnp.dot(tokens, w_query, preferred_element_type=jnp.float32).astype(jnp.bfloat16)
    keys = jnp.dot(tokens, w_key, preferred_element_type=jnp.float32).astype(jnp.bfloat16)
    values = jnp.dot(tokens, w_value, preferred_element_type=jnp.float32).astype(jnp.bfloat16)
    grad_attn = jnp.dot(d_out, w_out.T, preferred_element_type=jnp.float32).astype(jnp.bfloat16)
    query_blocks = query.reshape(NBLK, BLOCK, D)
    grad_blocks = grad_attn.reshape(NBLK, BLOCK, D)
    key_blocks = keys.reshape(NBLK, BLOCK, D)
    value_blocks = values.reshape(NBLK, BLOCK, D)
    remote = (jnp.arange(WSET, dtype=jnp.int32) >= BLK_DEV)[:, None, None]

    def per_owner(carry, owner):
        total_k, total_v = carry
        local = owner * BLK_DEV + jnp.arange(BLK_DEV, dtype=jnp.int32)
        fetched = (jnp.arange(N_OWNER, dtype=jnp.int32)[:, None] * BLK_DEV + fetch_list[owner]).reshape(-1)
        index = jnp.concatenate([local, fetched.astype(jnp.int32)])
        live_slots = (jnp.arange(CAP, dtype=jnp.int32)[None, :] < fetch_count[owner][:, None]).reshape(-1)
        alive_ws = jnp.concatenate([jnp.ones((BLK_DEV,), bool), live_slots])
        key_ws = key_blocks[index]
        value_ws = value_blocks[index]
        start = (owner * BLK_DEV).astype(jnp.int32)
        rows = lax.dynamic_slice_in_dim(pattern, start, BLK_DEV, 0)
        query_own = lax.dynamic_slice_in_dim(query_blocks, start, BLK_DEV, 0)
        grad_own = lax.dynamic_slice_in_dim(grad_blocks, start, BLK_DEV, 0)

        def per_query(inputs):
            entries, query_blk, grad_blk = inputs
            key_rows = key_ws[entries].reshape(KMAX * BLOCK, D)
            value_rows = value_ws[entries].reshape(KMAX * BLOCK, D)
            alive = jnp.repeat(alive_ws[entries], BLOCK)
            return attend(query_blk, grad_blk, key_rows, value_rows, alive)
        attended, grad_q, grad_k, grad_v = lax.map(per_query, (rows, query_own, grad_own))
        flat = rows.reshape(-1)
        part_k = jnp.zeros((WSET, BLOCK, D), jnp.float32).at[flat].add(grad_k.reshape(-1, BLOCK, D))
        part_v = jnp.zeros((WSET, BLOCK, D), jnp.float32).at[flat].add(grad_v.reshape(-1, BLOCK, D))
        part_k = jnp.where(remote, lax.optimization_barrier(part_k.astype(jnp.bfloat16)).astype(jnp.float32), part_k)
        part_v = jnp.where(remote, lax.optimization_barrier(part_v.astype(jnp.bfloat16)).astype(jnp.float32), part_v)
        total_k = total_k.at[index].add(part_k)
        total_v = total_v.at[index].add(part_v)
        return ((total_k, total_v), (attended, grad_q.astype(jnp.bfloat16)))
    init = (jnp.zeros((NBLK, BLOCK, D), jnp.float32), jnp.zeros((NBLK, BLOCK, D), jnp.float32))
    (total_k, total_v), (attended, grad_q) = lax.scan(per_owner, init, jnp.arange(N_OWNER, dtype=jnp.int32))
    attended = attended.reshape(TOKENS, D)
    grad_q = grad_q.reshape(TOKENS, D)
    grad_k = total_k.reshape(TOKENS, D).astype(jnp.bfloat16)
    grad_v = total_v.reshape(TOKENS, D).astype(jnp.bfloat16)
    grad_query = jnp.dot(tokens.T, grad_q, preferred_element_type=jnp.float32)
    grad_key = jnp.dot(tokens.T, grad_k, preferred_element_type=jnp.float32)
    grad_value = jnp.dot(tokens.T, grad_v, preferred_element_type=jnp.float32)
    grad_out = jnp.dot(attended.T, d_out, preferred_element_type=jnp.float32)
    d_tokens = (jnp.dot(grad_q, w_query.T, preferred_element_type=jnp.float32) + jnp.dot(grad_k, w_key.T, preferred_element_type=jnp.float32) + jnp.dot(grad_v, w_value.T, preferred_element_type=jnp.float32)).astype(jnp.bfloat16)
    return (d_tokens, grad_query, grad_key, grad_value, grad_out)
```

```python
import functools
import math

import jax
import jax.numpy as jnp
from jax import lax
from jax.experimental import pallas as pl
from jax.experimental.pallas import tpu as pltpu
from jax.sharding import PartitionSpec as P

HEAD_DIM = 64
BLOCK = 128
PAIR = 2 * HEAD_DIM
SCALE = 1.0 / math.sqrt(HEAD_DIM)
EXP2_SCALE = SCALE * math.log2(math.e)


def dot32(a, b):
    return jnp.dot(a, b, preferred_element_type=jnp.float32)


def split_heads(block):
    lane = lax.broadcasted_iota(jnp.int32, block.shape, 1)
    zero = jnp.zeros_like(block)
    return jnp.concatenate(
        [jnp.where(lane < HEAD_DIM, block, zero), jnp.where(lane < HEAD_DIM, zero, block)], axis=0
    )


def split_heads_t(block_t):
    zero = jnp.zeros((HEAD_DIM, BLOCK), block_t.dtype)
    return jnp.concatenate(
        [
            jnp.concatenate([block_t[:HEAD_DIM], zero], axis=1),
            jnp.concatenate([zero, block_t[HEAD_DIM:]], axis=1),
        ],
        axis=0,
    )


def own_columns(product):
    return jnp.concatenate([product[:HEAD_DIM, :BLOCK], product[HEAD_DIM:, BLOCK:]], axis=0)


def attention_back(
    blk_dev,
    kmax,
    pattern_ref,
    alive_ref,
    q_ref,
    g_ref,
    k_own_ref,
    v_own_ref,
    k_far_ref,
    v_far_ref,
    att_ref,
    gq_ref,
    ok_ref,
    ov_ref,
    fk_ref,
    fv_ref,
    k_ws,
    v_ws,
    kt_ws,
    vt_ws,
    acc_k,
    acc_v,
):
    b = pl.program_id(0)
    wset, _, width = k_ws.shape

    @pl.when(b == 0)
    def _():
        k_ws[:blk_dev] = k_own_ref[...]
        v_ws[:blk_dev] = v_own_ref[...]
        k_ws[blk_dev:] = k_far_ref[...]
        v_ws[blk_dev:] = v_far_ref[...]

        def turn(e, carry):
            kt_ws[e] = k_ws[e].T
            vt_ws[e] = v_ws[e].T
            acc_k[e] = jnp.zeros(acc_k.shape[1:], jnp.float32)
            acc_v[e] = jnp.zeros(acc_v.shape[1:], jnp.float32)
            return carry

        lax.fori_loop(0, wset, turn, 0)

    entries = [pattern_ref[b, i] for i in range(kmax)]
    bias = [jnp.where(alive_ref[e] > 0, 0.0, -1e30).astype(jnp.float32) for e in entries]
    for p in range(width // PAIR):
        cols = slice(p * PAIR, (p + 1) * PAIR)
        q = q_ref[:, cols]
        g = g_ref[:, cols]
        q_t = q.T
        g_t = g.T
        keys = jnp.concatenate([k_ws[e, :, cols] for e in entries], axis=0)
        scores = dot32(keys, split_heads_t(q_t))
        tiles = [scores[i * BLOCK : (i + 1) * BLOCK] for i in range(kmax)]
        top = None
        for tile, off in zip(tiles, bias):
            here = jnp.max(tile, axis=0, keepdims=True) * EXP2_SCALE + off
            top = here if top is None else jnp.maximum(top, here)
        tiles = [jnp.exp2(tile * EXP2_SCALE + (off - top)) for tile, off in zip(tiles, bias)]
        total = sum(jnp.sum(tile, axis=0, keepdims=True) for tile in tiles)
        probs = jnp.concatenate(tiles, axis=0) * (1.0 / total)
        probs_low = probs.astype(jnp.bfloat16)
        values_t = jnp.concatenate([vt_ws[e, cols, :] for e in entries], axis=1)
        att_t = own_columns(dot32(values_t, probs_low)).astype(jnp.bfloat16).astype(jnp.float32)
        att_ref[:, cols] = att_t.T.astype(jnp.bfloat16)
        hit = att_t * g_t.astype(jnp.float32)
        row_dot = jnp.concatenate(
            [
                jnp.sum(hit[:HEAD_DIM], axis=0, keepdims=True),
                jnp.sum(hit[HEAD_DIM:], axis=0, keepdims=True),
            ],
            axis=1,
        )
        values = jnp.concatenate([v_ws[e, :, cols] for e in entries], axis=0)
        grad_probs = dot32(values, split_heads_t(g_t))
        grad_scores = (probs * (grad_probs - row_dot)).astype(jnp.bfloat16)
        keys_t = jnp.concatenate([kt_ws[e, cols, :] for e in entries], axis=1)
        gq_t = own_columns(dot32(keys_t, grad_scores)) * SCALE
        gq_ref[:, cols] = gq_t.T.astype(jnp.bfloat16)
        part_k = dot32(grad_scores, split_heads(q))
        part_v = dot32(probs_low, split_heads(g))
        for i, e in enumerate(entries):
            rows = slice(i * BLOCK, (i + 1) * BLOCK)
            acc_k[e, :, cols] += part_k[rows]
            acc_v[e, :, cols] += part_v[rows]

    @pl.when(b == blk_dev - 1)
    def _():
        ok_ref[...] = acc_k[:blk_dev] * SCALE
        ov_ref[...] = acc_v[:blk_dev]
        fk_ref[...] = (acc_k[blk_dev:] * SCALE).astype(jnp.bfloat16)
        fv_ref[...] = acc_v[blk_dev:].astype(jnp.bfloat16)


def attention(pattern, alive, query, grad_attn, k_own, v_own, k_far, v_far):
    blk_dev, kmax = pattern.shape
    width = query.shape[1]
    slots = k_far.shape[0]
    wset = blk_dev + slots
    rows = pl.BlockSpec((BLOCK, width), lambda b, *_: (b, 0))
    whole = lambda n: pl.BlockSpec((n, BLOCK, width), lambda b, *_: (0, 0, 0))
    low = jnp.bfloat16
    full = jnp.float32
    return pl.pallas_call(
        functools.partial(attention_back, blk_dev, kmax),
        grid_spec=pltpu.PrefetchScalarGridSpec(
            num_scalar_prefetch=2,
            grid=(blk_dev,),
            in_specs=[rows, rows, whole(blk_dev), whole(blk_dev), whole(slots), whole(slots)],
            out_specs=[rows, rows, whole(blk_dev), whole(blk_dev), whole(slots), whole(slots)],
            scratch_shapes=[
                pltpu.VMEM((wset, BLOCK, width), low),
                pltpu.VMEM((wset, BLOCK, width), low),
                pltpu.VMEM((wset, width, BLOCK), low),
                pltpu.VMEM((wset, width, BLOCK), low),
                pltpu.VMEM((wset, BLOCK, width), full),
                pltpu.VMEM((wset, BLOCK, width), full),
            ],
        ),
        out_shape=[
            jax.ShapeDtypeStruct(query.shape, low),
            jax.ShapeDtypeStruct(query.shape, low),
            jax.ShapeDtypeStruct((blk_dev, BLOCK, width), full),
            jax.ShapeDtypeStruct((blk_dev, BLOCK, width), full),
            jax.ShapeDtypeStruct((slots, BLOCK, width), low),
            jax.ShapeDtypeStruct((slots, BLOCK, width), low),
        ],
        compiler_params=pltpu.CompilerParams(
            dimension_semantics=("arbitrary",), vmem_limit_bytes=56 * 2**20
        ),
        cost_estimate=pl.CostEstimate(
            flops=12 * blk_dev * BLOCK * kmax * BLOCK * width,
            bytes_accessed=20 * 2**20,
            transcendentals=blk_dev * BLOCK * kmax * BLOCK * (width // HEAD_DIM),
        ),
        name="attention_back",
    )(pattern, alive, query, grad_attn, k_own, v_own, k_far, v_far)


def on_device(tokens, d_out, w_query, w_key, w_value, w_out, fetch_list, fetch_count, pattern):
    blk_dev, kmax = pattern.shape
    cap = fetch_list.shape[2]
    width = w_query.shape[1]
    rows = tokens.shape[0]
    across = (((1,), (1,)), ((), ()))
    down = (((0,), (0,)), ((), ()))
    low = jnp.bfloat16
    swap = functools.partial(
        lax.all_to_all, axis_name="owner", split_axis=0, concat_axis=0, tiled=True
    )
    wanted = swap(fetch_list[0]).reshape(-1)
    keys_own = dot32(tokens, w_key).astype(low).reshape(blk_dev, BLOCK, width)
    k_far = swap(keys_own[wanted])
    values_own = dot32(tokens, w_value).astype(low).reshape(blk_dev, BLOCK, width)
    v_far = swap(values_own[wanted])
    query = dot32(tokens, w_query).astype(low)
    grad_attn = lax.dot_general(d_out, w_out, across, preferred_element_type=jnp.float32).astype(low)
    live = (jnp.arange(cap, dtype=jnp.int32)[None, :] < fetch_count[0][:, None]).reshape(-1)
    alive = jnp.concatenate([jnp.ones((blk_dev,), jnp.int32), live.astype(jnp.int32)])
    attended, grad_q, own_k, own_v, far_k, far_v = attention(
        pattern, alive, query, grad_attn, keys_own, values_own, k_far, v_far
    )
    back_k = swap(far_k)
    back_v = swap(far_v)
    term_o = lax.dot_general(attended, d_out, down, preferred_element_type=jnp.float32)
    term_q = lax.dot_general(tokens, grad_q, down, preferred_element_type=jnp.float32)
    owned = (jnp.arange(blk_dev, dtype=jnp.int32)[:, None] == wanted[None, :]).astype(low)

    def collect(own, back):
        far = jnp.einsum("ek,kbd->ebd", owned, back, preferred_element_type=jnp.float32)
        return (own + far).astype(low).reshape(rows, width)

    grad_k = collect(own_k, back_k)
    grad_v = collect(own_v, back_v)
    term_k = lax.dot_general(tokens, grad_k, down, preferred_element_type=jnp.float32)
    term_v = lax.dot_general(tokens, grad_v, down, preferred_element_type=jnp.float32)

    def owner_sum(term, axis):
        return lax.psum_scatter(
            term.astype(low), "owner", scatter_dimension=axis, tiled=True
        ).astype(jnp.float32)

    term_x = (
        lax.dot_general(grad_q, w_query, across, preferred_element_type=jnp.float32)
        + lax.dot_general(grad_k, w_key, across, preferred_element_type=jnp.float32)
        + lax.dot_general(grad_v, w_value, across, preferred_element_type=jnp.float32)
    )
    d_tokens = lax.psum_scatter(term_x.astype(low), "head", scatter_dimension=1, tiled=True)
    return (
        d_tokens,
        owner_sum(term_q, 0),
        owner_sum(term_k, 0),
        owner_sum(term_v, 0),
        owner_sum(term_o, 1),
    )


def solution(mesh):
    placed = (
        P(("groups", "owner"), None),
        P(("groups", "owner"), None),
        P(None, "head"),
        P(None, "head"),
        P(None, "head"),
        P("head", None),
        P(("groups", "owner"), None, None),
        P(("groups", "owner"), None),
        P(("groups", "owner"), None),
    )
    return jax.shard_map(
        on_device,
        mesh=mesh,
        in_specs=placed,
        out_specs=(
            P(("groups", "owner"), "head"),
            P(("groups", "owner"), "head"),
            P(("groups", "owner"), "head"),
            P(("groups", "owner"), "head"),
            P(("groups", "head"), "owner"),
        ),
        check_vma=False,
    )
```

```python
import functools
import math

import jax
import jax.numpy as jnp
from jax import lax
from jax.experimental import pallas as pl
from jax.experimental.pallas import tpu as pltpu
from jax.sharding import PartitionSpec as P

HEAD_DIM = 64
BLOCK = 128
PAIR = 2 * HEAD_DIM
SCALE = 1.0 / math.sqrt(HEAD_DIM)
EXP2_SCALE = SCALE * math.log2(math.e)


def dot32(a, b):
    return jnp.dot(a, b, preferred_element_type=jnp.float32)


def split_heads(block):
    lane = lax.broadcasted_iota(jnp.int32, block.shape, 1)
    zero = jnp.zeros_like(block)
    return jnp.concatenate(
        [jnp.where(lane < HEAD_DIM, block, zero), jnp.where(lane < HEAD_DIM, zero, block)], axis=0
    )


def split_heads_t(block_t):
    zero = jnp.zeros((HEAD_DIM, BLOCK), block_t.dtype)
    return jnp.concatenate(
        [
            jnp.concatenate([block_t[:HEAD_DIM], zero], axis=1),
            jnp.concatenate([zero, block_t[HEAD_DIM:]], axis=1),
        ],
        axis=0,
    )


def own_columns(product):
    return jnp.concatenate([product[:HEAD_DIM, :BLOCK], product[HEAD_DIM:, BLOCK:]], axis=0)


def attention_back(
    blk_dev,
    kmax,
    pattern_ref,
    alive_ref,
    q_ref,
    g_ref,
    k_own_ref,
    v_own_ref,
    k_far_ref,
    v_far_ref,
    att_ref,
    gq_ref,
    ok_ref,
    ov_ref,
    fk_ref,
    fv_ref,
    k_ws,
    v_ws,
    kt_ws,
    vt_ws,
    acc_k,
    acc_v,
):
    b = pl.program_id(0)
    wset, _, width = k_ws.shape

    @pl.when(b == 0)
    def _():
        k_ws[:blk_dev] = k_own_ref[...]
        v_ws[:blk_dev] = v_own_ref[...]
        k_ws[blk_dev:] = k_far_ref[...]
        v_ws[blk_dev:] = v_far_ref[...]

        def turn(e, carry):
            kt_ws[e] = k_ws[e].T
            vt_ws[e] = v_ws[e].T
            acc_k[e] = jnp.zeros(acc_k.shape[1:], jnp.float32)
            acc_v[e] = jnp.zeros(acc_v.shape[1:], jnp.float32)
            return carry

        lax.fori_loop(0, wset, turn, 0)

    entries = [pattern_ref[b, i] for i in range(kmax)]
    bias = [jnp.where(alive_ref[e] > 0, 0.0, -1e30).astype(jnp.float32) for e in entries]
    for p in range(width // PAIR):
        cols = slice(p * PAIR, (p + 1) * PAIR)
        q = q_ref[:, cols]
        g = g_ref[:, cols]
        q_t = q.T
        g_t = g.T
        keys = jnp.concatenate([k_ws[e, :, cols] for e in entries], axis=0)
        scores = dot32(keys, split_heads_t(q_t))
        tiles = [scores[i * BLOCK : (i + 1) * BLOCK] for i in range(kmax)]
        top = None
        for tile, off in zip(tiles, bias):
            here = jnp.max(tile, axis=0, keepdims=True) * EXP2_SCALE + off
            top = here if top is None else jnp.maximum(top, here)
        tiles = [jnp.exp2(tile * EXP2_SCALE + (off - top)) for tile, off in zip(tiles, bias)]
        total = sum(jnp.sum(tile, axis=0, keepdims=True) for tile in tiles)
        probs = jnp.concatenate(tiles, axis=0) * (1.0 / total)
        probs_low = probs.astype(jnp.bfloat16)
        values_t = jnp.concatenate([vt_ws[e, cols, :] for e in entries], axis=1)
        att_t = own_columns(dot32(values_t, probs_low)).astype(jnp.bfloat16).astype(jnp.float32)
        att_ref[:, cols] = att_t.T.astype(jnp.bfloat16)
        hit = att_t * g_t.astype(jnp.float32)
        row_dot = jnp.concatenate(
            [
                jnp.sum(hit[:HEAD_DIM], axis=0, keepdims=True),
                jnp.sum(hit[HEAD_DIM:], axis=0, keepdims=True),
            ],
            axis=1,
        )
        values = jnp.concatenate([v_ws[e, :, cols] for e in entries], axis=0)
        grad_probs = dot32(values, split_heads_t(g_t))
        grad_scores = (probs * (grad_probs - row_dot)).astype(jnp.bfloat16)
        keys_t = jnp.concatenate([kt_ws[e, cols, :] for e in entries], axis=1)
        gq_t = own_columns(dot32(keys_t, grad_scores)) * SCALE
        gq_ref[:, cols] = gq_t.T.astype(jnp.bfloat16)
        part_k = dot32(grad_scores, split_heads(q))
        part_v = dot32(probs_low, split_heads(g))
        for i, e in enumerate(entries):
            rows = slice(i * BLOCK, (i + 1) * BLOCK)
            acc_k[e, :, cols] += part_k[rows]
            acc_v[e, :, cols] += part_v[rows]

    @pl.when(b == blk_dev - 1)
    def _():
        ok_ref[...] = acc_k[:blk_dev] * SCALE
        ov_ref[...] = acc_v[:blk_dev]
        fk_ref[...] = (acc_k[blk_dev:] * SCALE).astype(jnp.bfloat16)
        fv_ref[...] = acc_v[blk_dev:].astype(jnp.bfloat16)


def attention(pattern, alive, query, grad_attn, k_own, v_own, k_far, v_far):
    blk_dev, kmax = pattern.shape
    width = query.shape[1]
    slots = k_far.shape[0]
    wset = blk_dev + slots
    rows = pl.BlockSpec((BLOCK, width), lambda b, *_: (b, 0))
    whole = lambda n: pl.BlockSpec((n, BLOCK, width), lambda b, *_: (0, 0, 0))
    low = jnp.bfloat16
    full = jnp.float32
    return pl.pallas_call(
        functools.partial(attention_back, blk_dev, kmax),
        grid_spec=pltpu.PrefetchScalarGridSpec(
            num_scalar_prefetch=2,
            grid=(blk_dev,),
            in_specs=[rows, rows, whole(blk_dev), whole(blk_dev), whole(slots), whole(slots)],
            out_specs=[rows, rows, whole(blk_dev), whole(blk_dev), whole(slots), whole(slots)],
            scratch_shapes=[
                pltpu.VMEM((wset, BLOCK, width), low),
                pltpu.VMEM((wset, BLOCK, width), low),
                pltpu.VMEM((wset, width, BLOCK), low),
                pltpu.VMEM((wset, width, BLOCK), low),
                pltpu.VMEM((wset, BLOCK, width), full),
                pltpu.VMEM((wset, BLOCK, width), full),
            ],
        ),
        out_shape=[
            jax.ShapeDtypeStruct(query.shape, low),
            jax.ShapeDtypeStruct(query.shape, low),
            jax.ShapeDtypeStruct((blk_dev, BLOCK, width), full),
            jax.ShapeDtypeStruct((blk_dev, BLOCK, width), full),
            jax.ShapeDtypeStruct((slots, BLOCK, width), low),
            jax.ShapeDtypeStruct((slots, BLOCK, width), low),
        ],
        compiler_params=pltpu.CompilerParams(
            dimension_semantics=("arbitrary",), vmem_limit_bytes=56 * 2**20
        ),
        cost_estimate=pl.CostEstimate(
            flops=12 * blk_dev * BLOCK * kmax * BLOCK * width,
            bytes_accessed=20 * 2**20,
            transcendentals=blk_dev * BLOCK * kmax * BLOCK * (width // HEAD_DIM),
        ),
        name="attention_back",
    )(pattern, alive, query, grad_attn, k_own, v_own, k_far, v_far)


CHUNKS = 4
TERMS = 4
MESH_ID = pl.DeviceIdType.MESH


def finish_sums(owners, heads, *refs):
    terms, (gq_ref, gk_ref, gv_ref, wq_ref, wk_ref, wv_ref) = refs[:TERMS], refs[TERMS : TERMS + 6]
    sums, dx_ref = refs[TERMS + 6 : 2 * TERMS + 6], refs[2 * TERMS + 6]
    (x_ref, near, mixed, far, got, near_send, near_recv, far_send, far_recv, got_send, got_recv) = refs[
        2 * TERMS + 7 :
    ]
    chips = heads // 2
    owner = lax.axis_index("owner")
    head = lax.axis_index("head")
    chip, core = head // 2, head % 2
    partner = chip * 2 + (1 - core)
    part = terms[0].shape[0] // owners
    rows, cols = dx_ref.shape
    step = rows // CHUNKS

    barrier = pltpu.get_barrier_semaphore()
    for off in range(1, owners):
        pl.semaphore_signal(
            barrier, inc=1, device_id={"owner": lax.rem(owner + off, owners)}, device_id_type=MESH_ID
        )
    pl.semaphore_signal(barrier, inc=1, device_id={"head": partner}, device_id_type=MESH_ID)
    for off in range(1, chips):
        pl.semaphore_signal(
            barrier,
            inc=1,
            device_id={"head": lax.rem(chip + off, chips) * 2 + core},
            device_id_type=MESH_ID,
        )
    pl.semaphore_wait(barrier, owners - 1 + 1 + chips - 1)

    sends = []
    for t in range(TERMS):
        for off in range(1, owners):
            to = lax.rem(owner + off, owners)
            copy = pltpu.make_async_remote_copy(
                src_ref=terms[t].at[pl.ds(pl.multiple_of(to * part, part), part)],
                dst_ref=got.at[t, off - 1],
                send_sem=got_send.at[t, off - 1],
                recv_sem=got_recv.at[t, off - 1],
                device_id={"owner": to},
                device_id_type=MESH_ID,
            )
            copy.start()
            sends.append(copy)

    weights = jnp.concatenate([wq_ref[...], wk_ref[...], wv_ref[...]], axis=1)
    near_copies = []
    for c in range(CHUNKS):
        here = slice(c * step, (c + 1) * step)
        grads = jnp.concatenate([gq_ref[here], gk_ref[here], gv_ref[here]], axis=1)
        for h in range(heads):
            x_ref[h, here] = lax.dot_general(
                grads,
                weights[h * cols : (h + 1) * cols],
                (((1,), (1,)), ((), ())),
                preferred_element_type=jnp.float32,
            ).astype(jnp.bfloat16)
        copies = []
        for j in range(chips):
            copy = pltpu.make_async_remote_copy(
                src_ref=x_ref.at[j * 2 + (1 - core), pl.ds(c * step, step)],
                dst_ref=near.at[j, pl.ds(c * step, step)],
                send_sem=near_send.at[c, j],
                recv_sem=near_recv.at[c, j],
                device_id={"head": partner},
                device_id_type=MESH_ID,
            )
            copy.start()
            copies.append(copy)
        near_copies.append(copies)

    far_copies = []
    for c in range(CHUNKS):
        here = slice(c * step, (c + 1) * step)
        for copy in near_copies[c]:
            copy.wait_recv()
        copies = []
        for off in range(1, chips):
            to = lax.rem(chip + off, chips)
            mixed[off - 1, here] = (
                x_ref[to * 2 + core, here].astype(jnp.float32)
                + near[to, here].astype(jnp.float32)
            ).astype(jnp.bfloat16)
            copy = pltpu.make_async_remote_copy(
                src_ref=mixed.at[off - 1, pl.ds(c * step, step)],
                dst_ref=far.at[off - 1, pl.ds(c * step, step)],
                send_sem=far_send.at[c, off - 1],
                recv_sem=far_recv.at[c, off - 1],
                device_id={"head": to * 2 + core},
                device_id_type=MESH_ID,
            )
            copy.start()
            copies.append(copy)
        far_copies.append(copies)

    for c in range(CHUNKS):
        here = slice(c * step, (c + 1) * step)
        total = x_ref[head, here].astype(jnp.float32) + near[chip, here].astype(jnp.float32)
        for off, copy in enumerate(far_copies[c]):
            copy.wait_recv()
            total += far[off, here].astype(jnp.float32)
        dx_ref[here] = total.astype(jnp.bfloat16)
    for t in range(TERMS):
        total = terms[t][pl.ds(pl.multiple_of(owner * part, part), part)].astype(jnp.float32)
        for off in range(owners - 1):
            sends[t * (owners - 1) + off].wait_recv()
            total += got[t, off].astype(jnp.float32)
        sums[t][...] = total
    for copy in sends:
        copy.wait_send()
    for copies in near_copies + far_copies:
        for copy in copies:
            copy.wait_send()


def finish(terms, grads, weights):
    owners = lax.axis_size("owner")
    heads = lax.axis_size("head")
    chips = heads // 2
    depth, width = terms[0].shape
    rows = grads[0].shape[0]
    part, cols = depth // owners, depth // heads
    low = jnp.bfloat16
    vmem = pl.BlockSpec(memory_space=pltpu.VMEM)
    return pl.pallas_call(
        functools.partial(finish_sums, owners, heads),
        out_shape=[jax.ShapeDtypeStruct((part, width), jnp.float32)] * TERMS
        + [jax.ShapeDtypeStruct((rows, cols), low)],
        in_specs=[vmem] * (TERMS + 6),
        out_specs=[vmem] * (TERMS + 1),
        scratch_shapes=[
            pltpu.VMEM((heads, rows, cols), low),
            pltpu.VMEM((chips, rows, cols), low),
            pltpu.VMEM((chips - 1, rows, cols), low),
            pltpu.VMEM((chips - 1, rows, cols), low),
            pltpu.VMEM((TERMS, owners - 1, part, width), low),
            pltpu.SemaphoreType.DMA((CHUNKS, chips)),
            pltpu.SemaphoreType.DMA((CHUNKS, chips)),
            pltpu.SemaphoreType.DMA((CHUNKS, chips - 1)),
            pltpu.SemaphoreType.DMA((CHUNKS, chips - 1)),
            pltpu.SemaphoreType.DMA((TERMS, owners - 1)),
            pltpu.SemaphoreType.DMA((TERMS, owners - 1)),
        ],
        compiler_params=pltpu.CompilerParams(
            collective_id=0, has_side_effects=True, vmem_limit_bytes=48 * 2**20
        ),
        cost_estimate=pl.CostEstimate(
            flops=6 * rows * depth * width, bytes_accessed=10 * 2**20, transcendentals=0
        ),
        name="finish_sums",
    )(*terms, *grads, *weights)


def on_device(tokens, d_out, w_query, w_key, w_value, w_out, fetch_list, fetch_count, pattern):
    blk_dev, kmax = pattern.shape
    cap = fetch_list.shape[2]
    width = w_query.shape[1]
    rows = tokens.shape[0]
    across = (((1,), (1,)), ((), ()))
    down = (((0,), (0,)), ((), ()))
    low = jnp.bfloat16
    swap = functools.partial(
        lax.all_to_all, axis_name="owner", split_axis=0, concat_axis=0, tiled=True
    )
    wanted = swap(fetch_list[0]).reshape(-1)
    keys_own = dot32(tokens, w_key).astype(low).reshape(blk_dev, BLOCK, width)
    k_far = swap(keys_own[wanted])
    values_own = dot32(tokens, w_value).astype(low).reshape(blk_dev, BLOCK, width)
    v_far = swap(values_own[wanted])
    query = dot32(tokens, w_query).astype(low)
    grad_attn = lax.dot_general(d_out, w_out, across, preferred_element_type=jnp.float32).astype(low)
    live = (jnp.arange(cap, dtype=jnp.int32)[None, :] < fetch_count[0][:, None]).reshape(-1)
    alive = jnp.concatenate([jnp.ones((blk_dev,), jnp.int32), live.astype(jnp.int32)])
    attended, grad_q, own_k, own_v, far_k, far_v = attention(
        pattern, alive, query, grad_attn, keys_own, values_own, k_far, v_far
    )
    back_k = swap(far_k)
    back_v = swap(far_v)
    def term(left, right):
        return lax.dot_general(left, right, down, preferred_element_type=jnp.float32).astype(low)

    term_o = term(d_out, attended)
    term_q = term(tokens, grad_q)
    owned = (jnp.arange(blk_dev, dtype=jnp.int32)[:, None] == wanted[None, :]).astype(low)

    def collect(own, back):
        far = jnp.einsum("ek,kbd->ebd", owned, back, preferred_element_type=jnp.float32)
        return (own + far).astype(low).reshape(rows, width)

    grad_k = collect(own_k, back_k)
    grad_v = collect(own_v, back_v)
    terms = (term_q, term(tokens, grad_k), term(tokens, grad_v), term_o)
    sum_q, sum_k, sum_v, sum_o, d_tokens = finish(
        terms, (grad_q, grad_k, grad_v), (w_query, w_key, w_value)
    )
    return (d_tokens, sum_q, sum_k, sum_v, sum_o.T)


def solution(mesh):
    placed = (
        P(("groups", "owner"), None),
        P(("groups", "owner"), None),
        P(None, "head"),
        P(None, "head"),
        P(None, "head"),
        P("head", None),
        P(("groups", "owner"), None, None),
        P(("groups", "owner"), None),
        P(("groups", "owner"), None),
    )
    return jax.shard_map(
        on_device,
        mesh=mesh,
        in_specs=placed,
        out_specs=(
            P(("groups", "owner"), "head"),
            P(("groups", "owner"), "head"),
            P(("groups", "owner"), "head"),
            P(("groups", "owner"), "head"),
            P(("groups", "head"), "owner"),
        ),
        check_vma=False,
    )
```

```python
import functools
import math

import jax
import jax.numpy as jnp
from jax import lax
from jax.experimental import pallas as pl
from jax.experimental.pallas import tpu as pltpu
from jax.sharding import PartitionSpec as P

HEAD_DIM = 64
BLOCK = 128
PAIR = 2 * HEAD_DIM
SCALE = 1.0 / math.sqrt(HEAD_DIM)
EXP2_SCALE = SCALE * math.log2(math.e)


def dot32(a, b):
    return jnp.dot(a, b, preferred_element_type=jnp.float32)


def split_heads(block):
    lane = lax.broadcasted_iota(jnp.int32, block.shape, 1)
    zero = jnp.zeros_like(block)
    return jnp.concatenate(
        [jnp.where(lane < HEAD_DIM, block, zero), jnp.where(lane < HEAD_DIM, zero, block)], axis=0
    )


def split_heads_t(block_t):
    zero = jnp.zeros((HEAD_DIM, BLOCK), block_t.dtype)
    return jnp.concatenate(
        [
            jnp.concatenate([block_t[:HEAD_DIM], zero], axis=1),
            jnp.concatenate([zero, block_t[HEAD_DIM:]], axis=1),
        ],
        axis=0,
    )


def own_columns(product):
    return jnp.concatenate([product[:HEAD_DIM, :BLOCK], product[HEAD_DIM:, BLOCK:]], axis=0)


def attention_back(
    blk_dev,
    kmax,
    pattern_ref,
    alive_ref,
    q_ref,
    g_ref,
    k_own_ref,
    v_own_ref,
    k_far_ref,
    v_far_ref,
    att_ref,
    gq_ref,
    ok_ref,
    ov_ref,
    fk_ref,
    fv_ref,
    k_ws,
    v_ws,
    kt_ws,
    vt_ws,
    acc_k,
    acc_v,
):
    b = pl.program_id(0)
    wset, _, width = k_ws.shape

    @pl.when(b == 0)
    def _():
        k_ws[:blk_dev] = k_own_ref[...]
        v_ws[:blk_dev] = v_own_ref[...]
        k_ws[blk_dev:] = k_far_ref[...]
        v_ws[blk_dev:] = v_far_ref[...]

        def turn(e, carry):
            kt_ws[e] = k_ws[e].T
            vt_ws[e] = v_ws[e].T
            acc_k[e] = jnp.zeros(acc_k.shape[1:], jnp.float32)
            acc_v[e] = jnp.zeros(acc_v.shape[1:], jnp.float32)
            return carry

        lax.fori_loop(0, wset, turn, 0)

    entries = [pattern_ref[b, i] for i in range(kmax)]
    bias = [jnp.where(alive_ref[e] > 0, 0.0, -1e30).astype(jnp.float32) for e in entries]
    for p in range(width // PAIR):
        cols = slice(p * PAIR, (p + 1) * PAIR)
        q = q_ref[:, cols]
        g = g_ref[:, cols]
        q_t = q.T
        g_t = g.T
        keys = jnp.concatenate([k_ws[e, :, cols] for e in entries], axis=0)
        scores = dot32(keys, split_heads_t(q_t))
        tiles = [scores[i * BLOCK : (i + 1) * BLOCK] for i in range(kmax)]
        top = None
        for tile, off in zip(tiles, bias):
            here = jnp.max(tile, axis=0, keepdims=True) * EXP2_SCALE + off
            top = here if top is None else jnp.maximum(top, here)
        tiles = [jnp.exp2(tile * EXP2_SCALE + (off - top)) for tile, off in zip(tiles, bias)]
        total = sum(jnp.sum(tile, axis=0, keepdims=True) for tile in tiles)
        probs = jnp.concatenate(tiles, axis=0) * (1.0 / total)
        probs_low = probs.astype(jnp.bfloat16)
        values_t = jnp.concatenate([vt_ws[e, cols, :] for e in entries], axis=1)
        att_t = own_columns(dot32(values_t, probs_low)).astype(jnp.bfloat16).astype(jnp.float32)
        att_ref[:, cols] = att_t.T.astype(jnp.bfloat16)
        hit = att_t * g_t.astype(jnp.float32)
        row_dot = jnp.concatenate(
            [
                jnp.sum(hit[:HEAD_DIM], axis=0, keepdims=True),
                jnp.sum(hit[HEAD_DIM:], axis=0, keepdims=True),
            ],
            axis=1,
        )
        values = jnp.concatenate([v_ws[e, :, cols] for e in entries], axis=0)
        grad_probs = dot32(values, split_heads_t(g_t))
        grad_scores = (probs * (grad_probs - row_dot)).astype(jnp.bfloat16)
        keys_t = jnp.concatenate([kt_ws[e, cols, :] for e in entries], axis=1)
        gq_t = own_columns(dot32(keys_t, grad_scores)) * SCALE
        gq_ref[:, cols] = gq_t.T.astype(jnp.bfloat16)
        part_k = dot32(grad_scores, split_heads(q))
        part_v = dot32(probs_low, split_heads(g))
        for i, e in enumerate(entries):
            rows = slice(i * BLOCK, (i + 1) * BLOCK)
            acc_k[e, :, cols] += part_k[rows]
            acc_v[e, :, cols] += part_v[rows]

    @pl.when(b == blk_dev - 1)
    def _():
        ok_ref[...] = acc_k[:blk_dev] * SCALE
        ov_ref[...] = acc_v[:blk_dev]
        fk_ref[...] = (acc_k[blk_dev:] * SCALE).astype(jnp.bfloat16)
        fv_ref[...] = acc_v[blk_dev:].astype(jnp.bfloat16)


def attention(pattern, alive, query, grad_attn, k_own, v_own, k_far, v_far):
    blk_dev, kmax = pattern.shape
    width = query.shape[1]
    slots = k_far.shape[0]
    wset = blk_dev + slots
    rows = pl.BlockSpec((BLOCK, width), lambda b, *_: (b, 0))
    whole = lambda n: pl.BlockSpec((n, BLOCK, width), lambda b, *_: (0, 0, 0))
    low = jnp.bfloat16
    full = jnp.float32
    return pl.pallas_call(
        functools.partial(attention_back, blk_dev, kmax),
        grid_spec=pltpu.PrefetchScalarGridSpec(
            num_scalar_prefetch=2,
            grid=(blk_dev,),
            in_specs=[rows, rows, whole(blk_dev), whole(blk_dev), whole(slots), whole(slots)],
            out_specs=[rows, rows, whole(blk_dev), whole(blk_dev), whole(slots), whole(slots)],
            scratch_shapes=[
                pltpu.VMEM((wset, BLOCK, width), low),
                pltpu.VMEM((wset, BLOCK, width), low),
                pltpu.VMEM((wset, width, BLOCK), low),
                pltpu.VMEM((wset, width, BLOCK), low),
                pltpu.VMEM((wset, BLOCK, width), full),
                pltpu.VMEM((wset, BLOCK, width), full),
            ],
        ),
        out_shape=[
            jax.ShapeDtypeStruct(query.shape, low),
            jax.ShapeDtypeStruct(query.shape, low),
            jax.ShapeDtypeStruct((blk_dev, BLOCK, width), full),
            jax.ShapeDtypeStruct((blk_dev, BLOCK, width), full),
            jax.ShapeDtypeStruct((slots, BLOCK, width), low),
            jax.ShapeDtypeStruct((slots, BLOCK, width), low),
        ],
        compiler_params=pltpu.CompilerParams(
            dimension_semantics=("arbitrary",), vmem_limit_bytes=56 * 2**20
        ),
        cost_estimate=pl.CostEstimate(
            flops=12 * blk_dev * BLOCK * kmax * BLOCK * width,
            bytes_accessed=20 * 2**20,
            transcendentals=blk_dev * BLOCK * kmax * BLOCK * (width // HEAD_DIM),
        ),
        name="attention_back",
    )(pattern, alive, query, grad_attn, k_own, v_own, k_far, v_far)


CHUNKS = 4
TERMS = 4
MESH_ID = pl.DeviceIdType.MESH


def finish_sums(owners, heads, *refs):
    (owned_ref, tokens_ref, d_out_ref, att_ref, gq_ref, own_k, own_v, far_k, far_v) = refs[:9]
    (wq_ref, wk_ref, wv_ref), sums, dx_ref = refs[9:12], refs[12 : 12 + TERMS], refs[12 + TERMS]
    (back, spread, gk_ref, gv_ref, terms, x_ref, near, mixed, far, got) = refs[13 + TERMS : 23 + TERMS]
    (back_send, back_recv, near_send, near_recv, far_send, far_recv, got_send, got_recv) = refs[
        23 + TERMS :
    ]
    chips = heads // 2
    owner = lax.axis_index("owner")
    head = lax.axis_index("head")
    chip, core = head // 2, head % 2
    partner = chip * 2 + (1 - core)
    depth, width = terms.shape[1:]
    part = depth // owners
    rows, cols = dx_ref.shape
    step = rows // CHUNKS
    blk_dev = own_k.shape[0]
    cap = back.shape[2]

    barrier = pltpu.get_barrier_semaphore()
    for off in range(1, owners):
        pl.semaphore_signal(
            barrier, inc=1, device_id={"owner": lax.rem(owner + off, owners)}, device_id_type=MESH_ID
        )
    pl.semaphore_signal(barrier, inc=1, device_id={"head": partner}, device_id_type=MESH_ID)
    for off in range(1, chips):
        pl.semaphore_signal(
            barrier,
            inc=1,
            device_id={"head": lax.rem(chip + off, chips) * 2 + core},
            device_id_type=MESH_ID,
        )
    pl.semaphore_wait(barrier, owners - 1 + 1 + chips - 1)

    back_copies = []
    for t, listed in enumerate((far_k, far_v)):
        for off in range(1, owners):
            to = lax.rem(owner + off, owners)
            copy = pltpu.make_async_remote_copy(
                src_ref=listed.at[pl.ds(to * cap, cap)],
                dst_ref=back.at[t, off],
                send_sem=back_send.at[t, off - 1],
                recv_sem=back_recv.at[t, off - 1],
                device_id={"owner": to},
                device_id_type=MESH_ID,
            )
            copy.start()
            back_copies.append(copy)
        back[t, 0] = listed[pl.ds(owner * cap, cap)]

    def make_term(t, left_ref, right_ref):
        turned = right_ref[...].T
        tile = min(depth, 256)
        for n in range(0, depth, tile):
            terms[t, n : n + tile] = dot32(turned, left_ref[:, n : n + tile]).T.astype(jnp.bfloat16)

    sends = [[] for _ in range(TERMS)]

    def send_term(t):
        for off in range(1, owners):
            to = lax.rem(owner + off, owners)
            copy = pltpu.make_async_remote_copy(
                src_ref=terms.at[t, pl.ds(pl.multiple_of(to * part, part), part)],
                dst_ref=got.at[t, off - 1],
                send_sem=got_send.at[t, off - 1],
                recv_sem=got_recv.at[t, off - 1],
                device_id={"owner": to},
                device_id_type=MESH_ID,
            )
            copy.start()
            sends[t].append(copy)

    make_term(0, tokens_ref, gq_ref)
    make_term(3, d_out_ref, att_ref)
    for copy in back_copies:
        copy.wait_recv()
    send_term(0)
    send_term(3)

    group = math.gcd(4, blk_dev)
    low = jnp.bfloat16
    one = (
        lax.broadcasted_iota(jnp.int32, (BLOCK, BLOCK), 0)
        == lax.broadcasted_iota(jnp.int32, (BLOCK, BLOCK), 1)
    ).astype(jnp.float32)
    arrived_k = back[0].reshape(owners * cap * BLOCK, width)
    arrived_v = back[1].reshape(owners * cap * BLOCK, width)
    for e0 in range(0, blk_dev, group):
        for e in range(group):
            for off in range(owners):
                source = lax.rem(owner + owners - off, owners)
                for c in range(cap):
                    at = (off * cap + c) * BLOCK
                    spread[e * BLOCK : (e + 1) * BLOCK, at : at + BLOCK] = (
                        one * owned_ref[e0 + e, source * cap + c]
                    ).astype(low)
        here = slice(e0 * BLOCK, (e0 + group) * BLOCK)
        for own, arrived, grad in ((own_k, arrived_k, gk_ref), (own_v, arrived_v, gv_ref)):
            local = own[e0 : e0 + group].reshape(group * BLOCK, width)
            grad[here] = (local + dot32(spread[...], arrived)).astype(low)

    weights = jnp.concatenate([wq_ref[...], wk_ref[...], wv_ref[...]], axis=1)
    near_copies = []
    for c in range(CHUNKS):
        here = slice(c * step, (c + 1) * step)
        grads = jnp.concatenate([gq_ref[here], gk_ref[here], gv_ref[here]], axis=1)
        for h in range(heads):
            x_ref[h, here] = lax.dot_general(
                grads,
                weights[h * cols : (h + 1) * cols],
                (((1,), (1,)), ((), ())),
                preferred_element_type=jnp.float32,
            ).astype(jnp.bfloat16)
        copies = []
        for j in range(chips):
            copy = pltpu.make_async_remote_copy(
                src_ref=x_ref.at[j * 2 + (1 - core), pl.ds(c * step, step)],
                dst_ref=near.at[j, pl.ds(c * step, step)],
                send_sem=near_send.at[c, j],
                recv_sem=near_recv.at[c, j],
                device_id={"head": partner},
                device_id_type=MESH_ID,
            )
            copy.start()
            copies.append(copy)
        near_copies.append(copies)
        if c == 0:
            make_term(1, tokens_ref, gk_ref)
            send_term(1)
        if c == 1:
            make_term(2, tokens_ref, gv_ref)
            send_term(2)

    far_copies = []
    for c in range(CHUNKS):
        here = slice(c * step, (c + 1) * step)
        for copy in near_copies[c]:
            copy.wait_recv()
        copies = []
        for off in range(1, chips):
            to = lax.rem(chip + off, chips)
            mixed[off - 1, here] = (
                x_ref[to * 2 + core, here].astype(jnp.float32)
                + near[to, here].astype(jnp.float32)
            ).astype(jnp.bfloat16)
            copy = pltpu.make_async_remote_copy(
                src_ref=mixed.at[off - 1, pl.ds(c * step, step)],
                dst_ref=far.at[off - 1, pl.ds(c * step, step)],
                send_sem=far_send.at[c, off - 1],
                recv_sem=far_recv.at[c, off - 1],
                device_id={"head": to * 2 + core},
                device_id_type=MESH_ID,
            )
            copy.start()
            copies.append(copy)
        far_copies.append(copies)

    for c in range(CHUNKS):
        here = slice(c * step, (c + 1) * step)
        total = x_ref[head, here].astype(jnp.float32) + near[chip, here].astype(jnp.float32)
        for off, copy in enumerate(far_copies[c]):
            copy.wait_recv()
            total += far[off, here].astype(jnp.float32)
        dx_ref[here] = total.astype(jnp.bfloat16)
    for t in range(TERMS):
        total = terms[t, pl.ds(pl.multiple_of(owner * part, part), part)].astype(jnp.float32)
        for off in range(owners - 1):
            sends[t][off].wait_recv()
            total += got[t, off].astype(jnp.float32)
        sums[t][...] = total
    for copy in back_copies:
        copy.wait_send()
    for copies in sends + near_copies + far_copies:
        for copy in copies:
            copy.wait_send()


def finish(owned, tokens, d_out, attended, grad_q, own, listed, weights):
    owners = lax.axis_size("owner")
    heads = lax.axis_size("head")
    chips = heads // 2
    rows, depth = tokens.shape
    width = grad_q.shape[1]
    slots = listed[0].shape[0]
    cap = slots // owners
    part, cols = depth // owners, depth // heads
    group = math.gcd(4, own[0].shape[0])
    low = jnp.bfloat16
    vmem = pl.BlockSpec(memory_space=pltpu.VMEM)
    pairs = lambda *shape: [pltpu.SemaphoreType.DMA(shape)] * 2
    return pl.pallas_call(
        functools.partial(finish_sums, owners, heads),
        out_shape=[jax.ShapeDtypeStruct((part, width), jnp.float32)] * TERMS
        + [jax.ShapeDtypeStruct((rows, cols), low)],
        in_specs=[pl.BlockSpec(memory_space=pltpu.SMEM)] + [vmem] * 11,
        out_specs=[vmem] * (TERMS + 1),
        scratch_shapes=[
            pltpu.VMEM((2, owners, cap, BLOCK, width), low),
            pltpu.VMEM((group * BLOCK, slots * BLOCK), low),
            pltpu.VMEM((rows, width), low),
            pltpu.VMEM((rows, width), low),
            pltpu.VMEM((TERMS, depth, width), low),
            pltpu.VMEM((heads, rows, cols), low),
            pltpu.VMEM((chips, rows, cols), low),
            pltpu.VMEM((chips - 1, rows, cols), low),
            pltpu.VMEM((chips - 1, rows, cols), low),
            pltpu.VMEM((TERMS, owners - 1, part, width), low),
        ]
        + pairs(2, owners - 1)
        + pairs(CHUNKS, chips)
        + pairs(CHUNKS, chips - 1)
        + pairs(TERMS, owners - 1),
        compiler_params=pltpu.CompilerParams(
            collective_id=0, has_side_effects=True, vmem_limit_bytes=56 * 2**20
        ),
        cost_estimate=pl.CostEstimate(
            flops=16 * rows * depth * width, bytes_accessed=20 * 2**20, transcendentals=0
        ),
        name="finish_sums",
    )(owned, tokens, d_out, attended, grad_q, *own, *listed, *weights)


def on_device(tokens, d_out, w_query, w_key, w_value, w_out, fetch_list, fetch_count, pattern):
    blk_dev, kmax = pattern.shape
    cap = fetch_list.shape[2]
    width = w_query.shape[1]
    across = (((1,), (1,)), ((), ()))
    low = jnp.bfloat16
    swap = functools.partial(
        lax.all_to_all, axis_name="owner", split_axis=0, concat_axis=0, tiled=True
    )
    wanted = swap(fetch_list[0]).reshape(-1)
    keys_own = dot32(tokens, w_key).astype(low).reshape(blk_dev, BLOCK, width)
    k_far = swap(keys_own[wanted])
    values_own = dot32(tokens, w_value).astype(low).reshape(blk_dev, BLOCK, width)
    v_far = swap(values_own[wanted])
    query = dot32(tokens, w_query).astype(low)
    grad_attn = lax.dot_general(d_out, w_out, across, preferred_element_type=jnp.float32).astype(low)
    live = (jnp.arange(cap, dtype=jnp.int32)[None, :] < fetch_count[0][:, None]).reshape(-1)
    alive = jnp.concatenate([jnp.ones((blk_dev,), jnp.int32), live.astype(jnp.int32)])
    attended, grad_q, own_k, own_v, far_k, far_v = attention(
        pattern, alive, query, grad_attn, keys_own, values_own, k_far, v_far
    )
    owned = jnp.arange(blk_dev, dtype=jnp.int32)[:, None] == wanted[None, :]
    sum_q, sum_k, sum_v, sum_o, d_tokens = finish(
        owned.astype(jnp.float32),
        tokens,
        d_out,
        attended,
        grad_q,
        (own_k, own_v),
        (far_k, far_v),
        (w_query, w_key, w_value),
    )
    return (d_tokens, sum_q, sum_k, sum_v, sum_o.T)


def solution(mesh):
    placed = (
        P(("groups", "owner"), None),
        P(("groups", "owner"), None),
        P(None, "head"),
        P(None, "head"),
        P(None, "head"),
        P("head", None),
        P(("groups", "owner"), None, None),
        P(("groups", "owner"), None),
        P(("groups", "owner"), None),
    )
    return jax.shard_map(
        on_device,
        mesh=mesh,
        in_specs=placed,
        out_specs=(
            P(("groups", "owner"), "head"),
            P(("groups", "owner"), "head"),
            P(("groups", "owner"), "head"),
            P(("groups", "owner"), "head"),
            P(("groups", "head"), "owner"),
        ),
        check_vma=False,
    )
```

```python
import functools
import math

import jax
import jax.numpy as jnp
from jax import lax
from jax.experimental import pallas as pl
from jax.experimental.pallas import tpu as pltpu
from jax.sharding import PartitionSpec as P

HEAD_DIM = 64
BLOCK = 128
PAIR = 2 * HEAD_DIM
SCALE = 1.0 / math.sqrt(HEAD_DIM)
EXP2_SCALE = SCALE * math.log2(math.e)


def dot32(a, b):
    return jnp.dot(a, b, preferred_element_type=jnp.float32)


def split_heads(block):
    lane = lax.broadcasted_iota(jnp.int32, block.shape, 1)
    zero = jnp.zeros_like(block)
    return jnp.concatenate(
        [jnp.where(lane < HEAD_DIM, block, zero), jnp.where(lane < HEAD_DIM, zero, block)], axis=0
    )


def split_heads_t(block_t):
    zero = jnp.zeros((HEAD_DIM, BLOCK), block_t.dtype)
    return jnp.concatenate(
        [
            jnp.concatenate([block_t[:HEAD_DIM], zero], axis=1),
            jnp.concatenate([zero, block_t[HEAD_DIM:]], axis=1),
        ],
        axis=0,
    )


def own_columns(product):
    return jnp.concatenate([product[:HEAD_DIM, :BLOCK], product[HEAD_DIM:, BLOCK:]], axis=0)


def attention_back(
    blk_dev,
    kmax,
    pattern_ref,
    alive_ref,
    q_ref,
    g_ref,
    own_ref,
    far_ref,
    att_ref,
    gq_ref,
    ok_ref,
    ov_ref,
    fk_ref,
    fv_ref,
    k_ws,
    v_ws,
    kt_ws,
    vt_ws,
    acc_k,
    acc_v,
):
    b = pl.program_id(0)
    wset, _, width = k_ws.shape

    @pl.when(b == 0)
    def _():
        k_ws[:blk_dev] = own_ref[:, :, :width]
        v_ws[:blk_dev] = own_ref[:, :, width:]
        k_ws[blk_dev:] = far_ref[:, :, :width]
        v_ws[blk_dev:] = far_ref[:, :, width:]

        def turn(e, carry):
            kt_ws[e] = k_ws[e].T
            vt_ws[e] = v_ws[e].T
            acc_k[e] = jnp.zeros(acc_k.shape[1:], jnp.float32)
            acc_v[e] = jnp.zeros(acc_v.shape[1:], jnp.float32)
            return carry

        lax.fori_loop(0, wset, turn, 0)

    entries = [pattern_ref[b, i] for i in range(kmax)]
    bias = [jnp.where(alive_ref[e] > 0, 0.0, -1e30).astype(jnp.float32) for e in entries]
    for p in range(width // PAIR):
        cols = slice(p * PAIR, (p + 1) * PAIR)
        q = q_ref[:, cols]
        g = g_ref[:, cols]
        q_t = q.T
        g_t = g.T
        keys = jnp.concatenate([k_ws[e, :, cols] for e in entries], axis=0)
        scores = dot32(keys, split_heads_t(q_t))
        tiles = [scores[i * BLOCK : (i + 1) * BLOCK] for i in range(kmax)]
        top = None
        for tile, off in zip(tiles, bias):
            here = jnp.max(tile, axis=0, keepdims=True) * EXP2_SCALE + off
            top = here if top is None else jnp.maximum(top, here)
        tiles = [jnp.exp2(tile * EXP2_SCALE + (off - top)) for tile, off in zip(tiles, bias)]
        total = sum(jnp.sum(tile, axis=0, keepdims=True) for tile in tiles)
        probs = jnp.concatenate(tiles, axis=0) * (1.0 / total)
        probs_low = probs.astype(jnp.bfloat16)
        values_t = jnp.concatenate([vt_ws[e, cols, :] for e in entries], axis=1)
        att_t = own_columns(dot32(values_t, probs_low)).astype(jnp.bfloat16).astype(jnp.float32)
        att_ref[:, cols] = att_t.T.astype(jnp.bfloat16)
        hit = att_t * g_t.astype(jnp.float32)
        row_dot = jnp.concatenate(
            [
                jnp.sum(hit[:HEAD_DIM], axis=0, keepdims=True),
                jnp.sum(hit[HEAD_DIM:], axis=0, keepdims=True),
            ],
            axis=1,
        )
        values = jnp.concatenate([v_ws[e, :, cols] for e in entries], axis=0)
        grad_probs = dot32(values, split_heads_t(g_t))
        grad_scores = (probs * (grad_probs - row_dot)).astype(jnp.bfloat16)
        keys_t = jnp.concatenate([kt_ws[e, cols, :] for e in entries], axis=1)
        gq_t = own_columns(dot32(keys_t, grad_scores)) * SCALE
        gq_ref[:, cols] = gq_t.T.astype(jnp.bfloat16)
        part_k = dot32(grad_scores, split_heads(q))
        part_v = dot32(probs_low, split_heads(g))
        for i, e in enumerate(entries):
            rows = slice(i * BLOCK, (i + 1) * BLOCK)
            acc_k[e, :, cols] += part_k[rows]
            acc_v[e, :, cols] += part_v[rows]

    @pl.when(b == blk_dev - 1)
    def _():
        ok_ref[...] = acc_k[:blk_dev] * SCALE
        ov_ref[...] = acc_v[:blk_dev]
        fk_ref[...] = (acc_k[blk_dev:] * SCALE).astype(jnp.bfloat16)
        fv_ref[...] = acc_v[blk_dev:].astype(jnp.bfloat16)


def attention(pattern, alive, query, grad_attn, own, far):
    blk_dev, kmax = pattern.shape
    width = query.shape[1]
    slots = far.shape[0]
    wset = blk_dev + slots
    rows = pl.BlockSpec((BLOCK, width), lambda b, *_: (b, 0))
    whole = lambda n: pl.BlockSpec((n, BLOCK, width), lambda b, *_: (0, 0, 0))
    both = lambda n: pl.BlockSpec((n, BLOCK, 2 * width), lambda b, *_: (0, 0, 0))
    low = jnp.bfloat16
    full = jnp.float32
    return pl.pallas_call(
        functools.partial(attention_back, blk_dev, kmax),
        grid_spec=pltpu.PrefetchScalarGridSpec(
            num_scalar_prefetch=2,
            grid=(blk_dev,),
            in_specs=[rows, rows, both(blk_dev), both(slots)],
            out_specs=[rows, rows, whole(blk_dev), whole(blk_dev), whole(slots), whole(slots)],
            scratch_shapes=[
                pltpu.VMEM((wset, BLOCK, width), low),
                pltpu.VMEM((wset, BLOCK, width), low),
                pltpu.VMEM((wset, width, BLOCK), low),
                pltpu.VMEM((wset, width, BLOCK), low),
                pltpu.VMEM((wset, BLOCK, width), full),
                pltpu.VMEM((wset, BLOCK, width), full),
            ],
        ),
        out_shape=[
            jax.ShapeDtypeStruct(query.shape, low),
            jax.ShapeDtypeStruct(query.shape, low),
            jax.ShapeDtypeStruct((blk_dev, BLOCK, width), full),
            jax.ShapeDtypeStruct((blk_dev, BLOCK, width), full),
            jax.ShapeDtypeStruct((slots, BLOCK, width), low),
            jax.ShapeDtypeStruct((slots, BLOCK, width), low),
        ],
        compiler_params=pltpu.CompilerParams(
            dimension_semantics=("arbitrary",), vmem_limit_bytes=56 * 2**20
        ),
        cost_estimate=pl.CostEstimate(
            flops=12 * blk_dev * BLOCK * kmax * BLOCK * width,
            bytes_accessed=20 * 2**20,
            transcendentals=blk_dev * BLOCK * kmax * BLOCK * (width // HEAD_DIM),
        ),
        name="attention_back",
    )(pattern, alive, query, grad_attn, own, far)


CHUNKS = 4
TERMS = 4
MESH_ID = pl.DeviceIdType.MESH


def finish_sums(owners, heads, *refs):
    (owned_ref, tokens_ref, d_out_ref, att_ref, gq_ref, own_k, own_v, far_k, far_v) = refs[:9]
    (wq_ref, wk_ref, wv_ref), sums, dx_ref = refs[9:12], refs[12 : 12 + TERMS], refs[12 + TERMS]
    (back, spread, gk_ref, gv_ref, terms, x_ref, near, mixed, far, got) = refs[13 + TERMS : 23 + TERMS]
    (back_send, back_recv, near_send, near_recv, far_send, far_recv, got_send, got_recv) = refs[
        23 + TERMS :
    ]
    chips = heads // 2
    owner = lax.axis_index("owner")
    head = lax.axis_index("head")
    chip, core = head // 2, head % 2
    partner = chip * 2 + (1 - core)
    depth, width = terms.shape[1:]
    part = depth // owners
    rows, cols = dx_ref.shape
    step = rows // CHUNKS
    blk_dev = own_k.shape[0]
    cap = back.shape[2]

    barrier = pltpu.get_barrier_semaphore()
    for off in range(1, owners):
        pl.semaphore_signal(
            barrier, inc=1, device_id={"owner": lax.rem(owner + off, owners)}, device_id_type=MESH_ID
        )
    pl.semaphore_signal(barrier, inc=1, device_id={"head": partner}, device_id_type=MESH_ID)
    for off in range(1, chips):
        pl.semaphore_signal(
            barrier,
            inc=1,
            device_id={"head": lax.rem(chip + off, chips) * 2 + core},
            device_id_type=MESH_ID,
        )
    pl.semaphore_wait(barrier, owners - 1 + 1 + chips - 1)

    back_copies = []
    for t, listed in enumerate((far_k, far_v)):
        for off in range(1, owners):
            to = lax.rem(owner + off, owners)
            copy = pltpu.make_async_remote_copy(
                src_ref=listed.at[pl.ds(to * cap, cap)],
                dst_ref=back.at[t, off],
                send_sem=back_send.at[t, off - 1],
                recv_sem=back_recv.at[t, off - 1],
                device_id={"owner": to},
                device_id_type=MESH_ID,
            )
            copy.start()
            back_copies.append(copy)
        back[t, 0] = listed[pl.ds(owner * cap, cap)]

    def make_term(t, left_ref, right_ref):
        turned = right_ref[...].T
        tile = min(depth, 256)
        for n in range(0, depth, tile):
            terms[t, n : n + tile] = dot32(turned, left_ref[:, n : n + tile]).T.astype(jnp.bfloat16)

    sends = [[] for _ in range(TERMS)]

    def send_term(t):
        for off in range(1, owners):
            to = lax.rem(owner + off, owners)
            copy = pltpu.make_async_remote_copy(
                src_ref=terms.at[t, pl.ds(pl.multiple_of(to * part, part), part)],
                dst_ref=got.at[t, off - 1],
                send_sem=got_send.at[t, off - 1],
                recv_sem=got_recv.at[t, off - 1],
                device_id={"owner": to},
                device_id_type=MESH_ID,
            )
            copy.start()
            sends[t].append(copy)

    make_term(0, tokens_ref, gq_ref)
    make_term(3, d_out_ref, att_ref)
    for copy in back_copies:
        copy.wait_recv()
    send_term(0)
    send_term(3)

    group = math.gcd(4, blk_dev)
    low = jnp.bfloat16
    one = (
        lax.broadcasted_iota(jnp.int32, (BLOCK, BLOCK), 0)
        == lax.broadcasted_iota(jnp.int32, (BLOCK, BLOCK), 1)
    ).astype(jnp.float32)
    arrived_k = back[0].reshape(owners * cap * BLOCK, width)
    arrived_v = back[1].reshape(owners * cap * BLOCK, width)
    for e0 in range(0, blk_dev, group):
        for e in range(group):
            for off in range(owners):
                source = lax.rem(owner + owners - off, owners)
                for c in range(cap):
                    at = (off * cap + c) * BLOCK
                    spread[e * BLOCK : (e + 1) * BLOCK, at : at + BLOCK] = (
                        one * owned_ref[e0 + e, source * cap + c]
                    ).astype(low)
        here = slice(e0 * BLOCK, (e0 + group) * BLOCK)
        for own, arrived, grad in ((own_k, arrived_k, gk_ref), (own_v, arrived_v, gv_ref)):
            local = own[e0 : e0 + group].reshape(group * BLOCK, width)
            grad[here] = (local + dot32(spread[...], arrived)).astype(low)

    weights = jnp.concatenate([wq_ref[...], wk_ref[...], wv_ref[...]], axis=1)
    near_copies = []
    for c in range(CHUNKS):
        here = slice(c * step, (c + 1) * step)
        grads = jnp.concatenate([gq_ref[here], gk_ref[here], gv_ref[here]], axis=1)
        for h in range(heads):
            x_ref[h, here] = lax.dot_general(
                grads,
                weights[h * cols : (h + 1) * cols],
                (((1,), (1,)), ((), ())),
                preferred_element_type=jnp.float32,
            ).astype(jnp.bfloat16)
        copies = []
        for j in range(chips):
            copy = pltpu.make_async_remote_copy(
                src_ref=x_ref.at[j * 2 + (1 - core), pl.ds(c * step, step)],
                dst_ref=near.at[j, pl.ds(c * step, step)],
                send_sem=near_send.at[c, j],
                recv_sem=near_recv.at[c, j],
                device_id={"head": partner},
                device_id_type=MESH_ID,
            )
            copy.start()
            copies.append(copy)
        near_copies.append(copies)
        if c == 0:
            make_term(1, tokens_ref, gk_ref)
            send_term(1)
        if c == 1:
            make_term(2, tokens_ref, gv_ref)
            send_term(2)

    far_copies = []
    for c in range(CHUNKS):
        here = slice(c * step, (c + 1) * step)
        for copy in near_copies[c]:
            copy.wait_recv()
        copies = []
        for off in range(1, chips):
            to = lax.rem(chip + off, chips)
            mixed[off - 1, here] = (
                x_ref[to * 2 + core, here].astype(jnp.float32)
                + near[to, here].astype(jnp.float32)
            ).astype(jnp.bfloat16)
            copy = pltpu.make_async_remote_copy(
                src_ref=mixed.at[off - 1, pl.ds(c * step, step)],
                dst_ref=far.at[off - 1, pl.ds(c * step, step)],
                send_sem=far_send.at[c, off - 1],
                recv_sem=far_recv.at[c, off - 1],
                device_id={"head": to * 2 + core},
                device_id_type=MESH_ID,
            )
            copy.start()
            copies.append(copy)
        far_copies.append(copies)

    for c in range(CHUNKS):
        here = slice(c * step, (c + 1) * step)
        total = x_ref[head, here].astype(jnp.float32) + near[chip, here].astype(jnp.float32)
        for off, copy in enumerate(far_copies[c]):
            copy.wait_recv()
            total += far[off, here].astype(jnp.float32)
        dx_ref[here] = total.astype(jnp.bfloat16)
    for t in range(TERMS):
        total = terms[t, pl.ds(pl.multiple_of(owner * part, part), part)].astype(jnp.float32)
        for off in range(owners - 1):
            sends[t][off].wait_recv()
            total += got[t, off].astype(jnp.float32)
        sums[t][...] = total
    for copy in back_copies:
        copy.wait_send()
    for copies in sends + near_copies + far_copies:
        for copy in copies:
            copy.wait_send()


def finish(owned, tokens, d_out, attended, grad_q, own, listed, weights):
    owners = lax.axis_size("owner")
    heads = lax.axis_size("head")
    chips = heads // 2
    rows, depth = tokens.shape
    width = grad_q.shape[1]
    slots = listed[0].shape[0]
    cap = slots // owners
    part, cols = depth // owners, depth // heads
    group = math.gcd(4, own[0].shape[0])
    low = jnp.bfloat16
    vmem = pl.BlockSpec(memory_space=pltpu.VMEM)
    pairs = lambda *shape: [pltpu.SemaphoreType.DMA(shape)] * 2
    return pl.pallas_call(
        functools.partial(finish_sums, owners, heads),
        out_shape=[jax.ShapeDtypeStruct((part, width), jnp.float32)] * TERMS
        + [jax.ShapeDtypeStruct((rows, cols), low)],
        in_specs=[pl.BlockSpec(memory_space=pltpu.SMEM)] + [vmem] * 11,
        out_specs=[vmem] * (TERMS + 1),
        scratch_shapes=[
            pltpu.VMEM((2, owners, cap, BLOCK, width), low),
            pltpu.VMEM((group * BLOCK, slots * BLOCK), low),
            pltpu.VMEM((rows, width), low),
            pltpu.VMEM((rows, width), low),
            pltpu.VMEM((TERMS, depth, width), low),
            pltpu.VMEM((heads, rows, cols), low),
            pltpu.VMEM((chips, rows, cols), low),
            pltpu.VMEM((chips - 1, rows, cols), low),
            pltpu.VMEM((chips - 1, rows, cols), low),
            pltpu.VMEM((TERMS, owners - 1, part, width), low),
        ]
        + pairs(2, owners - 1)
        + pairs(CHUNKS, chips)
        + pairs(CHUNKS, chips - 1)
        + pairs(TERMS, owners - 1),
        compiler_params=pltpu.CompilerParams(
            collective_id=0, has_side_effects=True, vmem_limit_bytes=56 * 2**20
        ),
        cost_estimate=pl.CostEstimate(
            flops=16 * rows * depth * width, bytes_accessed=20 * 2**20, transcendentals=0
        ),
        name="finish_sums",
    )(owned, tokens, d_out, attended, grad_q, *own, *listed, *weights)


def on_device(tokens, d_out, w_query, w_key, w_value, w_out, fetch_list, fetch_count, pattern):
    blk_dev, kmax = pattern.shape
    cap = fetch_list.shape[2]
    width = w_query.shape[1]
    across = (((1,), (1,)), ((), ()))
    low = jnp.bfloat16
    swap = functools.partial(
        lax.all_to_all, axis_name="owner", split_axis=0, concat_axis=0, tiled=True
    )
    wanted = swap(fetch_list[0]).reshape(-1)
    pair = dot32(tokens, jnp.concatenate([w_key, w_value], axis=1)).astype(low)
    pair = pair.reshape(blk_dev, BLOCK, 2 * width)
    pair_far = swap(pair[wanted])
    query = dot32(tokens, w_query).astype(low)
    grad_attn = lax.dot_general(d_out, w_out, across, preferred_element_type=jnp.float32).astype(low)
    live = (jnp.arange(cap, dtype=jnp.int32)[None, :] < fetch_count[0][:, None]).reshape(-1)
    alive = jnp.concatenate([jnp.ones((blk_dev,), jnp.int32), live.astype(jnp.int32)])
    attended, grad_q, own_k, own_v, far_k, far_v = attention(
        pattern, alive, query, grad_attn, pair, pair_far
    )
    owned = jnp.arange(blk_dev, dtype=jnp.int32)[:, None] == wanted[None, :]
    sum_q, sum_k, sum_v, sum_o, d_tokens = finish(
        owned.astype(jnp.float32),
        tokens,
        d_out,
        attended,
        grad_q,
        (own_k, own_v),
        (far_k, far_v),
        (w_query, w_key, w_value),
    )
    return (d_tokens, sum_q, sum_k, sum_v, sum_o.T)


def solution(mesh):
    placed = (
        P(("groups", "owner"), None),
        P(("groups", "owner"), None),
        P(None, "head"),
        P(None, "head"),
        P(None, "head"),
        P("head", None),
        P(("groups", "owner"), None, None),
        P(("groups", "owner"), None),
        P(("groups", "owner"), None),
    )
    return jax.shard_map(
        on_device,
        mesh=mesh,
        in_specs=placed,
        out_specs=(
            P(("groups", "owner"), "head"),
            P(("groups", "owner"), "head"),
            P(("groups", "owner"), "head"),
            P(("groups", "owner"), "head"),
            P(("groups", "head"), "owner"),
        ),
        check_vma=False,
    )
```
